32 devices in a mesh: pipe: 2 (over y), seq: 4 (over z), tensor: 4 (over x, core).
Axes of the slice: x: 2, y: 2, z: 4, core: 2. Of those that a mesh axis runs over, the one named last changes fastest.
Arguments:
- resid: bfloat16 [2, 2, 1024, 8192], P('pipe', None, 'seq', 'tensor'), may hold values from -16 to 16
- streams: bfloat16 [2, 2, 1024, 3, 8192], P('pipe', None, 'seq', None, 'tensor'), may hold values from -6 to 6
- filt: bfloat16 [7, 8192], P(None, 'tensor'), may hold values from -2 to 2
- q_gain: float32 [4096], P('tensor'), may hold values from 0.5 to 2
- k_gain: float32 [4096], P('tensor'), may hold values from 0.1 to 1.9
- out_weight: bfloat16 [4096, 8192], P('seq', 'tensor'), may hold values from -0.09375 to 0.09375
- contig_lengths: int32 [2, 4], replicated, may hold values from 1 to 512, 1024 in all within a row
Outputs:
- activations: bfloat16 [2, 2, 1024, 8192], P('pipe', None, 'seq', 'tensor')
The draws below stay inside these ranges and needn't reach their ends.
Inputs may be any that keep to these rules, and one draw needn't show every extreme that they name: `contig_lengths`: each micro-batch's contigs lie end to end in order and fill its 1024 tokens; in every micro-batch the longest is exactly 512 tokens.
All inputs are finite; a program needn't handle non-finite values.
Results may differ from the reference program's by a relative error of at most 0.0062.
Values may be sent and summed in bfloat16 or wider, within the bound.
A program may use at most 128 MiB of HBM per device.

```python
import math
import jax
import jax.numpy as jnp
import numpy as np
from jax import lax

D = 8192
HD = 128
H = 32
K = 7
MB = 2
TOK_DEV = 256
SPAN = 2
MOST = 512
L = 1024
NCONTIG = 4
N_PIPE = 2
N_SEQ = 4


def draw_resid(key, part):
    base_key = jax.random.fold_in(key, 0)
    base = jax.random.normal(base_key, (N_PIPE, MB, L, D), jnp.float32)
    return jnp.clip(base, -16.0, 16.0).astype(jnp.bfloat16)


def block_levels(stream_key, shape, cuts, smallest, top_value):
    level = 1.0
    for position, parts in cuts:
        heights = jax.random.uniform(jax.random.fold_in(jax.random.fold_in(stream_key, 6), position), (parts,), jnp.float32, smallest / len(cuts), top_value / len(cuts))
        level = level * jnp.repeat(jnp.exp(heights), shape[position] // parts).reshape((-1,) + (1,) * (len(shape) - 1 - position))
    return level


def profile(number_of, total, most, slope):
    portions = [(1 << 20) // math.isqrt(standing ** slope) + 1 for standing in range(2, number_of + 1)]
    rest, holding = total - most - (number_of - 1), [1] * (number_of - 1)
    while rest > 0:
        free = [i for i in range(number_of - 1) if holding[i] < most]
        mass, budget = sum([portions[i] for i in free]), rest
        for i in free:
            more = min(most - holding[i], max(1, budget * portions[i] // mass), rest)
            holding[i] = holding[i] + more
            rest = rest - more
    return np.array([most] + holding)


def uneven_parts(rng, count, total, most, lean):
    if count == 2:
        one = jax.random.randint(rng, (), max(1, total - most), min(most, total - 1) + 1)
        return jnp.stack([one, total - one])
    sizes = jnp.asarray(profile(count, total, most, lean), jnp.int32)
    pairs = (count - 1) // 2
    giver, receiver = sizes[1:1 + 2 * pairs:2], sizes[2:2 + 2 * pairs:2]
    margin = jnp.minimum(giver - 1, most - receiver)
    shifted = jax.random.randint(jax.random.fold_in(rng, 1), (pairs,), 0, 1 << 20) % (margin + 1)
    sizes = sizes.at[1:1 + 2 * pairs:2].set(giver - shifted).at[2:2 + 2 * pairs:2].set(receiver + shifted)
    return sizes[jax.random.permutation(jax.random.fold_in(rng, 2), count)]


def normal_values(rng, shape, scale, limit, shards=(), held_as=jnp.bfloat16):
    values = scale * jax.random.normal(rng, shape, jnp.float32)
    if shards:
        values = values * block_levels(rng, shape, shards, -0.22, 0.18)
    return jnp.clip(values, -limit, limit).astype(held_as)


def setup_inputs(seed: int = 0) -> dict:
    arg_keys = jax.random.split(jax.random.key(seed), 8)
    resid = draw_resid(jax.random.fold_in(arg_keys[7], 71), 0)
    streams = normal_values(arg_keys[1], (N_PIPE, MB, L, 3, D), 1.0, 6.0, ((0, 2), (2, 4), (4, 4)))
    filt = normal_values(arg_keys[2], (K, D), K ** -0.5, 2.0, ((1, 4),))
    q_gain = jnp.clip(jnp.exp(math.log(2.0) - 1.3862944 * jax.random.uniform(arg_keys[3], (H * HD,), jnp.float32) ** block_levels(arg_keys[3], (H * HD,), ((0, 4),), -0.2, 0.2)), 0.5, 2.0)
    k_gain = jnp.clip(1.0 + 0.18 * jax.random.normal(arg_keys[4], (H * HD,), jnp.float32), 0.1, 1.9)
    out_weight = normal_values(arg_keys[5], (H * HD, D), (H * HD) ** -0.5, 0.09375, ((0, 4), (1, 4)))
    contig_lengths = jax.vmap(lambda own: uneven_parts(own, NCONTIG, L, MOST, 2))(jax.random.split(arg_keys[6], MB)).reshape((MB, NCONTIG)).astype(jnp.int32)
    return {"resid": resid, "streams": streams, "filt": filt, "q_gain": q_gain, "k_gain": k_gain, "out_weight": out_weight, "contig_lengths": contig_lengths}


NEG_FILL = -1e30


def rounded(values):
    return lax.optimization_barrier(values.astype(jnp.bfloat16))


def segment_of(contig_ends, positions):
    return jnp.sum((contig_ends[:, None, :] <= positions[None, :, None]).astype(jnp.int32), axis=2)


def reference(resid, streams, filt, q_gain, k_gain, out_weight, contig_lengths):
    resid_own = resid[0]
    streams_own = streams[0]
    gated = rounded(streams_own[:, :, 0].astype(jnp.float32) * streams_own[:, :, 2].astype(jnp.float32))
    padded = jnp.pad(gated.astype(jnp.float32), ((0, 0), (K - 1, 0), (0, 0)))
    conv_out = jnp.zeros(resid_own.shape, jnp.float32)
    for offset in range(K):
        conv_out = conv_out + filt[offset].astype(jnp.float32) * padded[:, K - 1 - offset:K - 1 - offset + L]
    hidden = rounded(resid_own.astype(jnp.float32) + streams_own[:, :, 1].astype(jnp.float32) * conv_out)
    attend = hidden.reshape(MB, L, H, 2, HD)[:, :, :, 0].reshape(MB, L, H * HD)
    contig_ends = jnp.cumsum(contig_lengths, axis=1).astype(jnp.int32)
    window = SPAN * TOK_DEV
    queries = rounded(attend.astype(jnp.float32) * q_gain)
    keys = rounded(attend.astype(jnp.float32) * k_gain)
    keys_pad = jnp.pad(keys, ((0, 0), (window, 0), (0, 0)))
    values_pad = jnp.pad(attend, ((0, 0), (window, 0), (0, 0)))

    def one_block(index):
        start = (index * TOK_DEV).astype(jnp.int32)
        query_pos = start + jnp.arange(TOK_DEV, dtype=jnp.int32)
        key_pos = start - window + jnp.arange(window + TOK_DEV, dtype=jnp.int32)
        q_block = lax.dynamic_slice_in_dim(queries, start, TOK_DEV, 1).astype(jnp.float32).reshape(MB, TOK_DEV, H, HD)
        k_block = lax.dynamic_slice_in_dim(keys_pad, start, window + TOK_DEV, 1).astype(jnp.float32).reshape(MB, window + TOK_DEV, H, HD)
        v_block = lax.dynamic_slice_in_dim(values_pad, start, window + TOK_DEV, 1).astype(jnp.float32).reshape(MB, window + TOK_DEV, H, HD)
        same = segment_of(contig_ends, query_pos)[:, :, None] == segment_of(contig_ends, key_pos)[:, None, :]
        causal = (key_pos[None, None, :] <= query_pos[None, :, None]) & (key_pos[None, None, :] >= 0)
        visible = (same & causal)[:, None]
        scores = jnp.einsum('mthd,mshd->mhts', q_block, k_block) / HD
        scores = jnp.where(visible, scores, NEG_FILL)
        top = jnp.max(scores, axis=-1, keepdims=True)
        weights = jnp.where(visible, jnp.exp(scores - top), 0.0)
        total = jnp.sum(weights, axis=-1)
        mixed = jnp.einsum('mhts,mshd->mthd', rounded(weights).astype(jnp.float32), v_block)
        mixed = mixed / jnp.transpose(total, (0, 2, 1))[..., None]
        return mixed.astype(jnp.bfloat16).reshape(MB, TOK_DEV, H * HD)

    blocks = lax.map(one_block, jnp.arange(N_SEQ, dtype=jnp.int32))
    mixed = jnp.transpose(blocks, (1, 0, 2, 3)).reshape(MB * L, H * HD)
    projected = jnp.dot(mixed, out_weight, preferred_element_type=jnp.float32)
    projected = projected.astype(jnp.bfloat16).reshape(MB, L, D)
    return jnp.stack([hidden, projected])
```

```python
import functools

import jax
import jax.numpy as jnp
from jax import lax
from jax.experimental import pallas as pl
from jax.experimental.pallas import tpu as pltpu
from jax.sharding import PartitionSpec as P

HD = 128
MESH = pl.DeviceIdType.MESH
HALO = 16
PARTS = 4


NEG_FILL = -1e30


def from_behind(value, axis, steps):
    count = lax.axis_size(axis)
    first, last = (max(0, -steps), min(count, count - steps))
    return lax.ppermute(value, axis, [(source, source + steps) for source in range(first, last)])


def segment_of(contig_ends, positions):
    return jnp.sum((contig_ends[:, None, :] <= positions[None, :, None]).astype(jnp.int32), axis=2)


def weights_travel(resid, streams, filt, q_gain, k_gain, out_weight, contig_lengths):
    resid_own = resid[0]
    streams_own = streams[0]
    tap_count = filt.shape[0]
    batch_count = resid_own.shape[0]
    tok_rows = resid_own.shape[1]
    local_heads = q_gain.shape[0] // HD
    attend_width = local_heads * HD
    section_index = lax.axis_index("pipe")
    seq_index = lax.axis_index("seq")
    gated = (
        streams_own[:, :, 0].astype(jnp.float32) * streams_own[:, :, 2].astype(jnp.float32)
    ).astype(jnp.bfloat16)
    prev_rows = from_behind(gated[:, tok_rows - (tap_count - 1) :], "seq", 1)

    def run_hyena(operand):
        extended = jnp.concatenate([prev_rows, gated], axis=1)
        conv_out = jnp.zeros(resid_own.shape, jnp.float32)
        for offset in range(tap_count):
            begin = tap_count - 1 - offset
            conv_out = conv_out + filt[offset].astype(jnp.float32) * extended[
                :, begin : begin + tok_rows
            ].astype(jnp.float32)
        return (
            resid_own.astype(jnp.float32) + streams_own[:, :, 1].astype(jnp.float32) * conv_out
        ).astype(jnp.bfloat16)

    def no_hyena(operand):
        return jnp.zeros_like(resid_own)

    hidden = lax.cond(section_index == 0, run_hyena, no_hyena, 0)
    attend = hidden.reshape(batch_count, tok_rows, local_heads, 2, HD)[:, :, :, 0].reshape(
        batch_count, tok_rows, attend_width
    )
    arrived = from_behind(attend, "pipe", 1)
    contig_ends = jnp.cumsum(contig_lengths, axis=1)
    reach_span = min(4, lax.axis_size("seq") // 2)
    pieces = [arrived]
    for distance in range(1, reach_span + 1):
        pieces.insert(0, from_behind(arrived, "seq", distance))
    key_source = jnp.concatenate(pieces, axis=1)
    key_rows = (reach_span + 1) * tok_rows

    def run_attention(operand):
        query_pos = seq_index * tok_rows + jnp.arange(tok_rows, dtype=jnp.int32)
        key_pos = (seq_index - reach_span) * tok_rows + jnp.arange(key_rows, dtype=jnp.int32)
        same = (
            segment_of(contig_ends, query_pos)[:, :, None]
            == segment_of(contig_ends, key_pos)[:, None, :]
        )
        causal = (key_pos[None, None, :] <= query_pos[None, :, None]) & (
            key_pos[None, None, :] >= 0
        )
        visible = same & causal
        queries = (
            (arrived.astype(jnp.float32) * q_gain)
            .astype(jnp.bfloat16)
            .reshape(batch_count, tok_rows, local_heads, HD)
        )
        keys = (
            (key_source.astype(jnp.float32) * k_gain)
            .astype(jnp.bfloat16)
            .reshape(batch_count, key_rows, local_heads, HD)
        )
        values = key_source.reshape(batch_count, key_rows, local_heads, HD)

        def one_batch(items):
            query_part, key_part, value_part, visible_part = items
            scores = (
                jnp.einsum("thd,shd->hts", query_part, key_part, preferred_element_type=jnp.float32)
                / HD
            )
            scores = jnp.where(visible_part[None], scores, NEG_FILL)
            top = jnp.max(scores, axis=-1, keepdims=True)
            weights = jnp.where(visible_part[None], jnp.exp(scores - top), 0.0)
            total = jnp.sum(weights, axis=-1)
            mixed = jnp.einsum(
                "hts,shd->thd",
                weights.astype(jnp.bfloat16),
                value_part,
                preferred_element_type=jnp.float32,
            )
            mixed = mixed / jnp.transpose(total)[..., None]
            return mixed.astype(jnp.bfloat16).reshape(tok_rows, attend_width)

        return lax.map(one_batch, (queries, keys, values, visible))

    def no_attention(operand):
        return jnp.zeros_like(arrived)

    mixed = lax.cond(section_index == 1, run_attention, no_attention, 0)
    all_heads = lax.all_gather(mixed, "tensor", axis=2, tiled=True)
    flattened = all_heads.reshape(batch_count * tok_rows, all_heads.shape[2])
    projected = jnp.dot(
        flattened,
        lax.all_gather(out_weight, "seq", axis=0, tiled=True),
        preferred_element_type=jnp.float32,
    )
    attn_out = projected.astype(jnp.bfloat16).reshape(batch_count, tok_rows, out_weight.shape[1])
    output = jnp.where(section_index == 0, hidden, attn_out)
    return output[None]


def hyena_kernel(stream_ref, resid_ref, prev_ref, filt_ref, hidden_ref, attend_ref, extended):
    taps, rows, width = filt_ref.shape[0], resid_ref.shape[1], resid_ref.shape[2]
    gate, value = stream_ref[0, 0].astype(jnp.float32), stream_ref[0, 2].astype(jnp.float32)
    extended[:HALO] = prev_ref[0].astype(jnp.float32)
    extended[HALO:] = (gate * value).astype(jnp.bfloat16).astype(jnp.float32)
    step = 64
    for col in range(0, width, HD):
        lanes = slice(col, col + HD)
        tap_rows = [filt_ref[j : j + 1, lanes].astype(jnp.float32) for j in range(taps)]
        for row in range(0, rows, step):
            conv = jnp.zeros((step, HD), jnp.float32)
            for j in range(taps):
                begin = HALO + row - j
                conv = conv + tap_rows[j] * extended[begin : begin + step, lanes]
            own = slice(row, row + step)
            out_gate = stream_ref[0, 1, own, lanes].astype(jnp.float32)
            hidden = (resid_ref[0, own, lanes].astype(jnp.float32) + out_gate * conv).astype(jnp.bfloat16)
            hidden_ref[0, own, lanes] = hidden
            if col // HD % 2 == 0:
                attend_ref[0, 0, own, col // 2 : col // 2 + HD] = hidden


def run_hyena(streams, resid, prev, filt, pieces):
    batch, _, rows, width = streams.shape
    block = width // pieces
    return pl.pallas_call(
        hyena_kernel,
        grid=(batch, pieces),
        in_specs=[
            pl.BlockSpec((1, 3, rows, block), lambda m, k: (m, 0, 0, k)),
            pl.BlockSpec((1, rows, block), lambda m, k: (m, 0, k)),
            pl.BlockSpec((1, HALO, block), lambda m, k: (m, 0, k)),
            pl.BlockSpec((filt.shape[0], block), lambda m, k: (0, k)),
        ],
        out_specs=[
            pl.BlockSpec((1, rows, block), lambda m, k: (m, 0, k)),
            pl.BlockSpec((1, 1, rows, block // 2), lambda m, k: (m, k, 0, 0)),
        ],
        out_shape=[
            jax.ShapeDtypeStruct((batch, rows, width), jnp.bfloat16),
            jax.ShapeDtypeStruct((batch, pieces, rows, block // 2), jnp.bfloat16),
        ],
        scratch_shapes=[pltpu.VMEM((HALO + rows, block), jnp.float32)],
        compiler_params=pltpu.CompilerParams(vmem_limit_bytes=32 << 20),
        name="hyena",
    )(streams, resid, prev, filt)


def landed(ref, sem):
    pltpu.make_async_copy(ref, ref, sem).wait()


def attention_kernel(
    n_seq, n_tensor, rows, attend_ref, gains_ref, begin_ref, weight_ref, out_ref,
    tokens, gains, queries, keys, own_mixed, mixed, weight, partial,
    send_a, recv_a, send_b, recv_b, send_y, recv_y,
    tok_send, tok_recv, gain_send, gain_recv, weight_sem, mix_send, mix_recv, mix_local,
    a_send, a_recv, b_send, b_recv, y_send, y_recv,
):
    pipe, seq, tensor = (lax.axis_index(name) for name in ("pipe", "seq", "tensor"))
    piece = tokens.shape[1]
    half = seq // 2
    inner = seq + half * (3 - 2 * seq)
    me = (pipe * n_seq + seq) * n_tensor + tensor
    world = 2 * n_seq * n_tensor
    barrier = pltpu.get_barrier_semaphore()

    fetch = pltpu.make_async_copy(weight_ref, weight, weight_sem)
    fetch.start()

    def greet(step, carry):
        other = lax.rem(me + step, world)
        device = (other // (n_seq * n_tensor), other // n_tensor % n_seq, other % n_tensor)
        pl.semaphore_signal(barrier, inc=1, device_id=device, device_id_type=MESH)
        return carry

    lax.fori_loop(1, world, greet, 0)
    pl.semaphore_wait(barrier, world - 1)

    def remote(source, target, send_sem, recv_sem, device):
        return pltpu.make_async_remote_copy(
            src_ref=source, dst_ref=target, send_sem=send_sem, recv_sem=recv_sem,
            device_id=device, device_id_type=MESH,
        )

    def deliver(wait):
        for batch in range(2):
            for other in range(n_tensor):
                slot = batch * n_tensor + other
                is_self = (seq == tensor) & (other == tensor) if batch == 0 else None
                source = attend_ref.at[batch, other]
                target = tokens.at[pl.ds(pl.multiple_of(seq * rows, rows), rows)]
                far = remote(source, target, tok_send.at[slot], tok_recv.at[seq], (batch, tensor, other))
                gain_far = remote(gains_ref.at[other], gains, gain_send.at[slot], gain_recv.at[0], (batch, tensor, other))
                away = True if is_self is None else jnp.logical_not(is_self)

                @pl.when(away)
                def _():
                    far.wait_send() if wait else far.start()

                @pl.when(away & (seq == 0))
                def _():
                    gain_far.wait_send() if wait else gain_far.start()

                if is_self is not None and not wait:

                    @pl.when(is_self)
                    def _():
                        pltpu.make_async_copy(source, target, tok_recv.at[seq]).start()

                    @pl.when(is_self & (seq == 0))
                    def _():
                        pltpu.make_async_copy(gains_ref.at[other], gains, gain_recv.at[0]).start()

    @pl.when(pipe == 0)
    def _():
        deliver(False)

    landed(gains, gain_recv.at[0])
    for source in range(n_seq):
        here = slice(source * rows, (source + 1) * rows)
        landed(tokens.at[here], tok_recv.at[source])
        block = tokens[here].astype(jnp.float32)
        queries[here] = (block * gains[0:1]).astype(jnp.bfloat16)
        keys[here] = (block * gains[1:2]).astype(jnp.bfloat16)

    window = min(3, n_seq) * rows
    mine = pl.ds(pl.multiple_of(tensor * piece, piece), piece)

    def chunk_of(step):
        order = (3 - step) + (step // 2) * (inner * (2 * step - 5))
        return order + half * (3 - 2 * order)

    def mix_copy(step, hop):
        return remote(
            own_mixed.at[step], mixed.at[step, :, mine], mix_send.at[step, hop - 1],
            mix_recv.at[step, tensor], (pipe, seq, lax.rem(tensor + hop, n_tensor)),
        )

    def attention(step):
        chunk = chunk_of(step)
        first = pl.multiple_of(chunk * rows, rows)
        low = pl.multiple_of((chunk // 3) * rows, rows)
        position = first + lax.broadcasted_iota(jnp.int32, (rows, window), 0)
        key_position = low + lax.broadcasted_iota(jnp.int32, (rows, window), 1)
        visible = (key_position >= begin_ref[pl.ds(first, rows)]) & (key_position <= position)
        for head in range(piece // HD):
            lanes = slice(head * HD, (head + 1) * HD)
            scores = lax.dot_general(
                queries[pl.ds(first, rows), lanes], keys[pl.ds(low, window), lanes],
                (((1,), (1,)), ((), ())), preferred_element_type=jnp.float32,
            ) * (1.0 / HD)
            scores = jnp.where(visible, scores, NEG_FILL)
            weights = jnp.exp(scores - jnp.max(scores, axis=1, keepdims=True))
            total = jnp.sum(weights, axis=1, keepdims=True)
            result = jnp.dot(
                weights.astype(jnp.bfloat16), tokens[pl.ds(low, window), lanes],
                preferred_element_type=jnp.float32,
            )
            own_mixed[step, :, lanes] = (result / total).astype(jnp.bfloat16)
        pltpu.make_async_copy(own_mixed.at[step], mixed.at[step, :, mine], mix_local.at[step]).start()
        for hop in range(1, n_tensor):
            mix_copy(step, hop).start()

    def inward(step, part):
        return remote(
            send_a.at[step, part], recv_a.at[step, part], a_send.at[step, part],
            a_recv.at[step, part], (pipe, 1 + half, tensor),
        )

    def project(step):
        pltpu.make_async_copy(own_mixed.at[step], mixed.at[step, :, mine], mix_local.at[step]).wait()
        for hop in range(1, n_tensor):
            source = lax.rem(tensor + hop, n_tensor)
            lanes = pl.ds(pl.multiple_of(source * piece, piece), piece)
            landed(mixed.at[step, :, lanes], mix_recv.at[step, source])
        width = partial.shape[3]
        for part in range(PARTS):
            value = jnp.dot(
                mixed[step], weight[:, part * width : (part + 1) * width],
                preferred_element_type=jnp.float32,
            )
            partial[step, part] = value

            @pl.when((inner == 0) & (step < 3))
            def _():
                send_a[step, part] = value.astype(jnp.bfloat16)
                inward(step, part).start()

    def turn(step, carry):
        @pl.when(step < 4)
        def _():
            attention(step)

        @pl.when(step == 1)
        def _():
            fetch.wait()

        @pl.when(step > 0)
        def _():
            project(step - 1)

        return carry

    lax.fori_loop(0, 5, turn, 0)

    def across(step, part):
        return remote(
            send_a.at[step, part], recv_b.at[step, part], b_send.at[step, part],
            b_recv.at[step, part], (pipe, 3 - seq, tensor),
        )

    def outward(part):
        return remote(
            send_b.at[part], recv_b.at[0, part], b_send.at[2, part],
            b_recv.at[0, part], (pipe, 3 * half, tensor),
        )

    def home(part):
        return remote(
            send_y.at[part], recv_y.at[part], y_send.at[part], y_recv.at[part], (1, seq, tensor)
        )

    def finish(part, value):
        width = value.shape[1]

        @pl.when(pipe == 0)
        def _():
            send_y[part] = value.astype(jnp.bfloat16)
            home(part).start()

        @pl.when(pipe == 1)
        def _():
            out_ref[1, :, part * width : (part + 1) * width] = value.astype(jnp.bfloat16)

    def forward(step, part):
        landed(recv_a.at[step, part], a_recv.at[step, part])
        send_a[step, part] = (partial[step, part] + recv_a[step, part].astype(jnp.float32)).astype(jnp.bfloat16)
        across(step, part).start()

    def relay(part):
        landed(recv_b.at[0, part], b_recv.at[0, part])
        send_b[part] = (partial[2, part] + recv_b[0, part].astype(jnp.float32)).astype(jnp.bfloat16)
        outward(part).start()

    @pl.when(inner == 1)
    def _():
        for part in range(PARTS):
            forward(0, part)
            if part > 0:
                relay(part - 1)
        relay(PARTS - 1)
        for part in range(PARTS):
            forward(1, part)
        for part in range(PARTS):
            landed(recv_a.at[2, part], a_recv.at[2, part])
            landed(recv_b.at[1, part], b_recv.at[1, part])
            finish(part, partial[3, part] + recv_a[2, part].astype(jnp.float32) + recv_b[1, part].astype(jnp.float32))
        for part in range(PARTS):
            across(0, part).wait_send()
            across(1, part).wait_send()
            outward(part).wait_send()

    @pl.when(inner == 0)
    def _():
        for part in range(PARTS):
            landed(recv_b.at[0, part], b_recv.at[0, part])
            finish(part, partial[3, part] + recv_b[0, part].astype(jnp.float32))
        for step in range(3):
            for part in range(PARTS):
                inward(step, part).wait_send()

    @pl.when(pipe == 1)
    def _():
        width = recv_y.shape[2]
        for part in range(PARTS):
            landed(recv_y.at[part], y_recv.at[part])
            out_ref[0, :, part * width : (part + 1) * width] = recv_y[part]

    @pl.when(pipe == 0)
    def _():
        for part in range(PARTS):
            home(part).wait_send()
        deliver(True)

    for step in range(4):
        for hop in range(1, n_tensor):
            mix_copy(step, hop).wait_send()


def run_attention(attend, gains, begins, weight, n_seq, n_tensor):
    batch, pieces, rows, piece = attend.shape
    depth, width = weight.shape
    length = n_seq * rows
    part = width // PARTS
    bf16, f32 = jnp.bfloat16, jnp.float32
    dma = pltpu.SemaphoreType.DMA
    anywhere, vmem = pl.BlockSpec(memory_space=pl.ANY), pl.BlockSpec(memory_space=pltpu.VMEM)
    return pl.pallas_call(
        functools.partial(attention_kernel, n_seq, n_tensor, rows),
        in_specs=[anywhere, anywhere, vmem, anywhere],
        out_specs=vmem,
        out_shape=jax.ShapeDtypeStruct((batch, rows, width), bf16),
        scratch_shapes=[
            pltpu.VMEM((length, piece), bf16),
            pltpu.VMEM(gains.shape[1:], f32),
            pltpu.VMEM((length, piece), bf16),
            pltpu.VMEM((length, piece), bf16),
            pltpu.VMEM((4, rows, piece), bf16),
            pltpu.VMEM((4, rows, depth), bf16),
            pltpu.VMEM((depth, width), bf16),
            pltpu.VMEM((4, PARTS, rows, part), f32),
            pltpu.VMEM((3, PARTS, rows, part), bf16),
            pltpu.VMEM((3, PARTS, rows, part), bf16),
            pltpu.VMEM((PARTS, rows, part), bf16),
            pltpu.VMEM((2, PARTS, rows, part), bf16),
            pltpu.VMEM((PARTS, rows, part), bf16),
            pltpu.VMEM((PARTS, rows, part), bf16),
            dma((2 * n_tensor,)), dma((n_seq,)), dma((2 * n_tensor,)), dma((1,)), dma,
            dma((4, n_tensor - 1)), dma((4, n_tensor)), dma((4,)),
            dma((3, PARTS)), dma((3, PARTS)), dma((3, PARTS)), dma((2, PARTS)),
            dma((PARTS,)), dma((PARTS,)),
        ],
        compiler_params=pltpu.CompilerParams(
            collective_id=0, has_side_effects=True, vmem_limit_bytes=56 << 20
        ),
        name="attention_projection",
    )(attend, gains, begins, weight)


def sums_travel(resid, streams, filt, q_gain, k_gain, out_weight, contig_lengths):
    n_seq, n_tensor = lax.axis_size("seq"), lax.axis_size("tensor")
    section = lax.axis_index("pipe")
    batch, rows = resid.shape[1:3]
    tail = streams[0, :, rows - HALO :].astype(jnp.float32)
    prev = from_behind((tail[:, :, 0] * tail[:, :, 2]).astype(jnp.bfloat16), "seq", 1)
    hidden, attend = run_hyena(
        jnp.transpose(streams[0], (0, 2, 1, 3)), resid[0], prev, filt, n_tensor
    )
    gains = jnp.stack([q_gain.reshape(n_tensor, -1), k_gain.reshape(n_tensor, -1)], axis=1)
    gains = jnp.pad(gains, ((0, 0), (0, 6), (0, 0)))
    ends = jnp.cumsum(jnp.where(section == 0, contig_lengths[0], contig_lengths[1]))
    position = jnp.arange(n_seq * rows, dtype=jnp.int32)
    begins = jnp.max(jnp.where(ends[None] <= position[:, None], ends[None], 0), axis=1, keepdims=True)
    projected = run_attention(attend, gains, begins.astype(jnp.int32), out_weight, n_seq, n_tensor)
    return jnp.where(section == 0, hidden, projected)[None]


def solution(mesh):
    few = mesh.shape["seq"] == 4 and mesh.shape["tensor"] == 4 and mesh.shape["pipe"] == 2
    per_device = sums_travel if few else weights_travel
    placed = (
        P("pipe", None, "seq", "tensor"),
        P("pipe", None, "seq", None, "tensor"),
        P(None, "tensor"),
        P("tensor"),
        P("tensor"),
        P("seq", "tensor"),
        P(),
    )
    return jax.shard_map(
        per_device,
        mesh=mesh,
        in_specs=placed,
        out_specs=P("pipe", None, "seq", "tensor"),
        check_vma=False,
    )
```

```python
import functools

import jax
import jax.numpy as jnp
from jax import lax
from jax.experimental import pallas as pl
from jax.experimental.pallas import tpu as pltpu
from jax.sharding import PartitionSpec as P

HD = 128
MESH = pl.DeviceIdType.MESH
HALO = 16
PARTS = 8


NEG_FILL = -1e30


def from_behind(value, axis, steps):
    count = lax.axis_size(axis)
    first, last = (max(0, -steps), min(count, count - steps))
    return lax.ppermute(value, axis, [(source, source + steps) for source in range(first, last)])


def segment_of(contig_ends, positions):
    return jnp.sum((contig_ends[:, None, :] <= positions[None, :, None]).astype(jnp.int32), axis=2)


def weights_travel(resid, streams, filt, q_gain, k_gain, out_weight, contig_lengths):
    resid_own = resid[0]
    streams_own = streams[0]
    tap_count = filt.shape[0]
    batch_count = resid_own.shape[0]
    tok_rows = resid_own.shape[1]
    local_heads = q_gain.shape[0] // HD
    attend_width = local_heads * HD
    section_index = lax.axis_index("pipe")
    seq_index = lax.axis_index("seq")
    gated = (
        streams_own[:, :, 0].astype(jnp.float32) * streams_own[:, :, 2].astype(jnp.float32)
    ).astype(jnp.bfloat16)
    prev_rows = from_behind(gated[:, tok_rows - (tap_count - 1) :], "seq", 1)

    def run_hyena(operand):
        extended = jnp.concatenate([prev_rows, gated], axis=1)
        conv_out = jnp.zeros(resid_own.shape, jnp.float32)
        for offset in range(tap_count):
            begin = tap_count - 1 - offset
            conv_out = conv_out + filt[offset].astype(jnp.float32) * extended[
                :, begin : begin + tok_rows
            ].astype(jnp.float32)
        return (
            resid_own.astype(jnp.float32) + streams_own[:, :, 1].astype(jnp.float32) * conv_out
        ).astype(jnp.bfloat16)

    def no_hyena(operand):
        return jnp.zeros_like(resid_own)

    hidden = lax.cond(section_index == 0, run_hyena, no_hyena, 0)
    attend = hidden.reshape(batch_count, tok_rows, local_heads, 2, HD)[:, :, :, 0].reshape(
        batch_count, tok_rows, attend_width
    )
    arrived = from_behind(attend, "pipe", 1)
    contig_ends = jnp.cumsum(contig_lengths, axis=1)
    reach_span = min(4, lax.axis_size("seq") // 2)
    pieces = [arrived]
    for distance in range(1, reach_span + 1):
        pieces.insert(0, from_behind(arrived, "seq", distance))
    key_source = jnp.concatenate(pieces, axis=1)
    key_rows = (reach_span + 1) * tok_rows

    def run_attention(operand):
        query_pos = seq_index * tok_rows + jnp.arange(tok_rows, dtype=jnp.int32)
        key_pos = (seq_index - reach_span) * tok_rows + jnp.arange(key_rows, dtype=jnp.int32)
        same = (
            segment_of(contig_ends, query_pos)[:, :, None]
            == segment_of(contig_ends, key_pos)[:, None, :]
        )
        causal = (key_pos[None, None, :] <= query_pos[None, :, None]) & (
            key_pos[None, None, :] >= 0
        )
        visible = same & causal
        queries = (
            (arrived.astype(jnp.float32) * q_gain)
            .astype(jnp.bfloat16)
            .reshape(batch_count, tok_rows, local_heads, HD)
        )
        keys = (
            (key_source.astype(jnp.float32) * k_gain)
            .astype(jnp.bfloat16)
            .reshape(batch_count, key_rows, local_heads, HD)
        )
        values = key_source.reshape(batch_count, key_rows, local_heads, HD)

        def one_batch(items):
            query_part, key_part, value_part, visible_part = items
            scores = (
                jnp.einsum("thd,shd->hts", query_part, key_part, preferred_element_type=jnp.float32)
                / HD
            )
            scores = jnp.where(visible_part[None], scores, NEG_FILL)
            top = jnp.max(scores, axis=-1, keepdims=True)
            weights = jnp.where(visible_part[None], jnp.exp(scores - top), 0.0)
            total = jnp.sum(weights, axis=-1)
            mixed = jnp.einsum(
                "hts,shd->thd",
                weights.astype(jnp.bfloat16),
                value_part,
                preferred_element_type=jnp.float32,
            )
            mixed = mixed / jnp.transpose(total)[..., None]
            return mixed.astype(jnp.bfloat16).reshape(tok_rows, attend_width)

        return lax.map(one_batch, (queries, keys, values, visible))

    def no_attention(operand):
        return jnp.zeros_like(arrived)

    mixed = lax.cond(section_index == 1, run_attention, no_attention, 0)
    all_heads = lax.all_gather(mixed, "tensor", axis=2, tiled=True)
    flattened = all_heads.reshape(batch_count * tok_rows, all_heads.shape[2])
    projected = jnp.dot(
        flattened,
        lax.all_gather(out_weight, "seq", axis=0, tiled=True),
        preferred_element_type=jnp.float32,
    )
    attn_out = projected.astype(jnp.bfloat16).reshape(batch_count, tok_rows, out_weight.shape[1])
    output = jnp.where(section_index == 0, hidden, attn_out)
    return output[None]


def landed(ref, sem):
    pltpu.make_async_copy(ref, ref, sem).wait()


def attention_kernel(
    n_seq, n_tensor, rows, streams_ref, resid_ref, filt_ref, gains_ref, begin_ref, weight_ref, out_ref,
    streams, resid, tail, tail_gated, prev, extended, attend,
    tokens, gains, queries, keys, own_mixed, mixed, weight, partial,
    send_a, recv_a, send_b, recv_b, send_y, recv_y,
    stream_sem, resid_sem, tail_sem, prev_send, prev_recv,
    tok_send, tok_recv, gain_send, gain_recv, weight_sem, mix_send, mix_recv, mix_local,
    a_send, a_recv, b_send, b_recv, y_send, y_recv,
):
    pipe, seq, tensor = (lax.axis_index(name) for name in ("pipe", "seq", "tensor"))
    piece = tokens.shape[1]
    half = seq // 2
    inner = seq + half * (3 - 2 * seq)
    me = (pipe * n_seq + seq) * n_tensor + tensor
    world = 2 * n_seq * n_tensor
    barrier = pltpu.get_barrier_semaphore()

    fetch = pltpu.make_async_copy(weight_ref, weight, weight_sem)
    fetch_tail = pltpu.make_async_copy(streams_ref.at[:, :, pl.ds(rows - HALO, HALO)], tail, tail_sem)

    def fetch_stream(batch):
        return pltpu.make_async_copy(streams_ref.at[batch], streams.at[batch], stream_sem.at[batch])

    def fetch_resid(batch):
        return pltpu.make_async_copy(resid_ref.at[batch], resid.at[batch], resid_sem.at[batch])

    @pl.when(pipe == 0)
    def _():
        fetch_tail.start()
        for batch in (1, 0):
            fetch_stream(batch).start()
            fetch_resid(batch).start()

    fetch.start()

    def greet(step, carry):
        other = lax.rem(me + step, world)
        device = (other // (n_seq * n_tensor), other // n_tensor % n_seq, other % n_tensor)
        pl.semaphore_signal(barrier, inc=1, device_id=device, device_id_type=MESH)
        return carry

    lax.fori_loop(1, world, greet, 0)
    pl.semaphore_wait(barrier, world - 1)

    def remote(source, target, send_sem, recv_sem, device):
        return pltpu.make_async_remote_copy(
            src_ref=source, dst_ref=target, send_sem=send_sem, recv_sem=recv_sem,
            device_id=device, device_id_type=MESH,
        )

    def to_head_rows(turn):
        batch, other = 1 - turn // n_tensor, turn % n_tensor
        here = tokens.at[pl.ds(pl.multiple_of(seq * rows, rows), rows)]
        device = (batch, tensor, other)
        is_self = (batch == 0) & (seq == tensor) & (other == tensor)
        return is_self, other, (
            attend.at[batch, other], here, tok_send.at[turn], tok_recv.at[seq], device
        ), (gains_ref.at[other], gains, gain_send.at[turn], gain_recv.at[0], device)

    def send_turn(turn):
        is_self, other, block, gain = to_head_rows(turn)

        @pl.when(jnp.logical_not(is_self))
        def _():
            remote(*block).start()

        @pl.when(jnp.logical_not(is_self) & (seq == 0))
        def _():
            remote(*gain).start()

        @pl.when(is_self)
        def _():
            pltpu.make_async_copy(block[0], block[1], block[3]).start()

        @pl.when(is_self & (seq == 0))
        def _():
            pltpu.make_async_copy(gain[0], gain[1], gain[3]).start()

    def wait_turn(turn, carry):
        is_self, other, block, gain = to_head_rows(turn)

        @pl.when(jnp.logical_not(is_self))
        def _():
            remote(*block).wait_send()

        @pl.when(jnp.logical_not(is_self) & (seq == 0))
        def _():
            remote(*gain).wait_send()

        return carry

    def send_prev():
        return remote(tail_gated, prev, prev_send, prev_recv, (0, seq + 1, tensor))

    def hyena(batch, column, keep):
        lanes = pl.ds(pl.multiple_of(column, HD), HD)
        taps = [filt_ref[j : j + 1, lanes].astype(jnp.float32) for j in range(filt_ref.shape[0])]
        step = 64
        for row in range(0, rows, step):
            conv = jnp.zeros((step, HD), jnp.float32)
            for j, tap in enumerate(taps):
                conv = conv + tap * extended[batch, pl.ds(HALO + row - j, step), lanes]
            own = pl.ds(row, step)
            out_gate = streams[batch, 1, own, lanes].astype(jnp.float32)
            hidden = resid[batch, own, lanes].astype(jnp.float32) + out_gate * conv
            hidden = hidden.astype(jnp.bfloat16)
            out_ref[batch, own, lanes] = hidden
            keep(own, hidden)

    @pl.when(pipe == 0)
    def _():
        fetch_tail.wait()
        tail_gated[...] = (
            tail[:, 0].astype(jnp.float32) * tail[:, 2].astype(jnp.float32)
        ).astype(jnp.bfloat16)

        @pl.when(seq < n_seq - 1)
        def _():
            send_prev().start()

        for batch in (1, 0):
            fetch_stream(batch).wait()

            def gate(strip, carry):
                own = pl.ds(pl.multiple_of(strip * 16, 16), 16)
                here = pl.ds(pl.multiple_of(HALO + strip * 16, 16), 16)
                gated = streams[batch, 0, own].astype(jnp.float32) * streams[batch, 2, own].astype(jnp.float32)
                extended[batch, here] = gated.astype(jnp.bfloat16).astype(jnp.float32)
                return carry

            lax.fori_loop(0, rows // 16, gate, 0)

        @pl.when(seq == 0)
        def _():
            extended[:, :HALO] = jnp.zeros((2, HALO, extended.shape[2]), jnp.float32)

        @pl.when(seq > 0)
        def _():
            landed(prev, prev_recv)
            extended[:, :HALO] = prev[...].astype(jnp.float32)

        for batch in (1, 0):
            fetch_resid(batch).wait()

        def attended(turn, carry):
            batch, other = 1 - turn // n_tensor, turn % n_tensor
            for head in range(piece // HD):

                def keep(own, hidden):
                    attend[batch, other, own, head * HD : (head + 1) * HD] = hidden

                hyena(batch, (other * (piece // HD) + head) * 2 * HD, keep)
            send_turn(turn)
            return carry

        def unattended(turn, carry):
            batch, other = 1 - turn // n_tensor, turn % n_tensor
            for head in range(piece // HD):
                hyena(batch, (other * (piece // HD) + head) * 2 * HD + HD, lambda own, hidden: None)
            return carry

        lax.fori_loop(0, 2 * n_tensor, attended, 0)
        lax.fori_loop(0, 2 * n_tensor, unattended, 0)

    landed(gains, gain_recv.at[0])
    for source in range(n_seq):
        here = slice(source * rows, (source + 1) * rows)
        landed(tokens.at[here], tok_recv.at[source])
        block = tokens[here].astype(jnp.float32)
        queries[here] = (block * gains[0:1]).astype(jnp.bfloat16)
        keys[here] = (block * gains[1:2]).astype(jnp.bfloat16)

    window = min(3, n_seq) * rows
    mine = pl.ds(pl.multiple_of(tensor * piece, piece), piece)

    def chunk_of(step):
        order = (3 - step) + (step // 2) * (inner * (2 * step - 5))
        return order + half * (3 - 2 * order)

    def mix_copy(step, hop):
        return remote(
            own_mixed.at[step], mixed.at[step, :, mine], mix_send.at[step, hop - 1],
            mix_recv.at[step, tensor], (pipe, seq, lax.rem(tensor + hop, n_tensor)),
        )

    def attention(step):
        chunk = chunk_of(step)
        first = pl.multiple_of(chunk * rows, rows)
        low = pl.multiple_of((chunk // 3) * rows, rows)
        position = first + lax.broadcasted_iota(jnp.int32, (rows, window), 0)
        key_position = low + lax.broadcasted_iota(jnp.int32, (rows, window), 1)
        visible = (key_position >= begin_ref[pl.ds(first, rows)]) & (key_position <= position)
        for head in range(piece // HD):
            lanes = slice(head * HD, (head + 1) * HD)
            scores = lax.dot_general(
                queries[pl.ds(first, rows), lanes], keys[pl.ds(low, window), lanes],
                (((1,), (1,)), ((), ())), preferred_element_type=jnp.float32,
            ) * (1.0 / HD)
            scores = jnp.where(visible, scores, NEG_FILL)
            weights = jnp.exp(scores - jnp.max(scores, axis=1, keepdims=True))
            total = jnp.sum(weights, axis=1, keepdims=True)
            result = jnp.dot(
                weights.astype(jnp.bfloat16), tokens[pl.ds(low, window), lanes],
                preferred_element_type=jnp.float32,
            )
            own_mixed[step, :, lanes] = (result / total).astype(jnp.bfloat16)
        pltpu.make_async_copy(own_mixed.at[step], mixed.at[step, :, mine], mix_local.at[step]).start()
        for hop in range(1, n_tensor):
            mix_copy(step, hop).start()

    def inward(step, part):
        return remote(
            send_a.at[step, part], recv_a.at[step, part], a_send.at[step, part],
            a_recv.at[step, part], (pipe, 1 + half, tensor),
        )

    def project(step):
        pltpu.make_async_copy(own_mixed.at[step], mixed.at[step, :, mine], mix_local.at[step]).wait()
        for hop in range(1, n_tensor):
            source = lax.rem(tensor + hop, n_tensor)
            lanes = pl.ds(pl.multiple_of(source * piece, piece), piece)
            landed(mixed.at[step, :, lanes], mix_recv.at[step, source])
        width = partial.shape[3]
        for part in range(PARTS):
            value = jnp.dot(
                mixed[step], weight[:, part * width : (part + 1) * width],
                preferred_element_type=jnp.float32,
            )
            partial[step, part] = value

            @pl.when((inner == 0) & (step < 3))
            def _():
                send_a[step, part] = value.astype(jnp.bfloat16)
                inward(step, part).start()

    def turn(step, carry):
        @pl.when(step < 4)
        def _():
            attention(step)

        @pl.when(step == 1)
        def _():
            fetch.wait()

        @pl.when(step > 0)
        def _():
            project(step - 1)

        return carry

    lax.fori_loop(0, 5, turn, 0)

    def across(step, part):
        return remote(
            send_a.at[step, part], recv_b.at[step, part], b_send.at[step, part],
            b_recv.at[step, part], (pipe, 3 - seq, tensor),
        )

    def outward(part):
        return remote(
            send_b.at[part], recv_b.at[0, part], b_send.at[2, part],
            b_recv.at[0, part], (pipe, 3 * half, tensor),
        )

    def home(part):
        return remote(
            send_y.at[part], recv_y.at[part], y_send.at[part], y_recv.at[part], (1, seq, tensor)
        )

    def finish(part, value):
        width = value.shape[1]

        @pl.when(pipe == 0)
        def _():
            send_y[part] = value.astype(jnp.bfloat16)
            home(part).start()

        @pl.when(pipe == 1)
        def _():
            out_ref[1, :, part * width : (part + 1) * width] = value.astype(jnp.bfloat16)

    def forward(step, part):
        landed(recv_a.at[step, part], a_recv.at[step, part])
        send_a[step, part] = (partial[step, part] + recv_a[step, part].astype(jnp.float32)).astype(jnp.bfloat16)
        across(step, part).start()

    def relay(part):
        landed(recv_b.at[0, part], b_recv.at[0, part])
        send_b[part] = (partial[2, part] + recv_b[0, part].astype(jnp.float32)).astype(jnp.bfloat16)
        outward(part).start()

    @pl.when(inner == 1)
    def _():
        for part in range(PARTS):
            forward(0, part)
            if part > 0:
                relay(part - 1)
        relay(PARTS - 1)
        for part in range(PARTS):
            forward(1, part)
        for part in range(PARTS):
            landed(recv_a.at[2, part], a_recv.at[2, part])
            landed(recv_b.at[1, part], b_recv.at[1, part])
            finish(part, partial[3, part] + recv_a[2, part].astype(jnp.float32) + recv_b[1, part].astype(jnp.float32))
        for part in range(PARTS):
            across(0, part).wait_send()
            across(1, part).wait_send()
            outward(part).wait_send()

    @pl.when(inner == 0)
    def _():
        for part in range(PARTS):
            landed(recv_b.at[0, part], b_recv.at[0, part])
            finish(part, partial[3, part] + recv_b[0, part].astype(jnp.float32))
        for step in range(3):
            for part in range(PARTS):
                inward(step, part).wait_send()

    @pl.when(pipe == 1)
    def _():
        width = recv_y.shape[2]
        for part in range(PARTS):
            landed(recv_y.at[part], y_recv.at[part])
            out_ref[0, :, part * width : (part + 1) * width] = recv_y[part]

    @pl.when(pipe == 0)
    def _():
        for part in range(PARTS):
            home(part).wait_send()
        lax.fori_loop(0, 2 * n_tensor, wait_turn, 0)

        @pl.when(seq < n_seq - 1)
        def _():
            send_prev().wait_send()

    for step in range(4):
        for hop in range(1, n_tensor):
            mix_copy(step, hop).wait_send()


def run_sections(streams, resid, filt, gains, begins, weight, n_seq, n_tensor):
    batch, rows = resid.shape[:2]
    piece = gains.shape[2]
    depth, width = weight.shape
    length = n_seq * rows
    part = width // PARTS
    bf16, f32 = jnp.bfloat16, jnp.float32
    dma = pltpu.SemaphoreType.DMA
    anywhere, vmem = pl.BlockSpec(memory_space=pl.ANY), pl.BlockSpec(memory_space=pltpu.VMEM)
    return pl.pallas_call(
        functools.partial(attention_kernel, n_seq, n_tensor, rows),
        in_specs=[anywhere, anywhere, vmem, anywhere, vmem, anywhere],
        out_specs=vmem,
        out_shape=jax.ShapeDtypeStruct((batch, rows, width), bf16),
        scratch_shapes=[
            pltpu.VMEM(streams.shape, bf16),
            pltpu.VMEM(resid.shape, bf16),
            pltpu.VMEM((batch, 3, HALO, width), bf16),
            pltpu.VMEM((batch, HALO, width), bf16),
            pltpu.VMEM((batch, HALO, width), bf16),
            pltpu.VMEM((batch, HALO + rows, width), f32),
            pltpu.VMEM((batch, n_tensor, rows, piece), bf16),
            pltpu.VMEM((length, piece), bf16),
            pltpu.VMEM(gains.shape[1:], f32),
            pltpu.VMEM((length, piece), bf16),
            pltpu.VMEM((length, piece), bf16),
            pltpu.VMEM((4, rows, piece), bf16),
            pltpu.VMEM((4, rows, depth), bf16),
            pltpu.VMEM((depth, width), bf16),
            pltpu.VMEM((4, PARTS, rows, part), f32),
            pltpu.VMEM((3, PARTS, rows, part), bf16),
            pltpu.VMEM((3, PARTS, rows, part), bf16),
            pltpu.VMEM((PARTS, rows, part), bf16),
            pltpu.VMEM((2, PARTS, rows, part), bf16),
            pltpu.VMEM((PARTS, rows, part), bf16),
            pltpu.VMEM((PARTS, rows, part), bf16),
            dma((batch,)), dma((batch,)), dma, dma, dma,
            dma((2 * n_tensor,)), dma((n_seq,)), dma((2 * n_tensor,)), dma((1,)), dma,
            dma((4, n_tensor - 1)), dma((4, n_tensor)), dma((4,)),
            dma((3, PARTS)), dma((3, PARTS)), dma((3, PARTS)), dma((2, PARTS)),
            dma((PARTS,)), dma((PARTS,)),
        ],
        compiler_params=pltpu.CompilerParams(
            collective_id=0, has_side_effects=True, vmem_limit_bytes=56 << 20
        ),
        name="sections",
    )(streams, resid, filt, gains, begins, weight)


def sums_travel(resid, streams, filt, q_gain, k_gain, out_weight, contig_lengths):
    n_seq, n_tensor = lax.axis_size("seq"), lax.axis_size("tensor")
    section = lax.axis_index("pipe")
    rows = resid.shape[2]
    gains = jnp.stack([q_gain.reshape(n_tensor, -1), k_gain.reshape(n_tensor, -1)], axis=1)
    gains = jnp.pad(gains, ((0, 0), (0, 6), (0, 0)))
    ends = jnp.cumsum(jnp.where(section == 0, contig_lengths[0], contig_lengths[1]))
    position = jnp.arange(n_seq * rows, dtype=jnp.int32)
    begins = jnp.max(jnp.where(ends[None] <= position[:, None], ends[None], 0), axis=1, keepdims=True)
    return run_sections(
        jnp.transpose(streams[0], (0, 2, 1, 3)), resid[0], filt, gains, begins.astype(jnp.int32),
        out_weight, n_seq, n_tensor,
    )[None]


def solution(mesh):
    few = mesh.shape["seq"] == 4 and mesh.shape["tensor"] == 4 and mesh.shape["pipe"] == 2
    per_device = sums_travel if few else weights_travel
    placed = (
        P("pipe", None, "seq", "tensor"),
        P("pipe", None, "seq", None, "tensor"),
        P(None, "tensor"),
        P("tensor"),
        P("tensor"),
        P("seq", "tensor"),
        P(),
    )
    return jax.shard_map(
        per_device,
        mesh=mesh,
        in_specs=placed,
        out_specs=P("pipe", None, "seq", "tensor"),
        check_vma=False,
    )
```

```python
import functools

import jax
import jax.numpy as jnp
from jax import lax
from jax.experimental import pallas as pl
from jax.experimental.pallas import tpu as pltpu
from jax.sharding import PartitionSpec as P

HD = 128
MESH = pl.DeviceIdType.MESH
HALO = 16
PARTS = 8


NEG_FILL = -1e30


def from_behind(value, axis, steps):
    count = lax.axis_size(axis)
    first, last = (max(0, -steps), min(count, count - steps))
    return lax.ppermute(value, axis, [(source, source + steps) for source in range(first, last)])


def segment_of(contig_ends, positions):
    return jnp.sum((contig_ends[:, None, :] <= positions[None, :, None]).astype(jnp.int32), axis=2)


def weights_travel(resid, streams, filt, q_gain, k_gain, out_weight, contig_lengths):
    resid_own = resid[0]
    streams_own = streams[0]
    tap_count = filt.shape[0]
    batch_count = resid_own.shape[0]
    tok_rows = resid_own.shape[1]
    local_heads = q_gain.shape[0] // HD
    attend_width = local_heads * HD
    section_index = lax.axis_index("pipe")
    seq_index = lax.axis_index("seq")
    gated = (
        streams_own[:, :, 0].astype(jnp.float32) * streams_own[:, :, 2].astype(jnp.float32)
    ).astype(jnp.bfloat16)
    prev_rows = from_behind(gated[:, tok_rows - (tap_count - 1) :], "seq", 1)

    def run_hyena(operand):
        extended = jnp.concatenate([prev_rows, gated], axis=1)
        conv_out = jnp.zeros(resid_own.shape, jnp.float32)
        for offset in range(tap_count):
            begin = tap_count - 1 - offset
            conv_out = conv_out + filt[offset].astype(jnp.float32) * extended[
                :, begin : begin + tok_rows
            ].astype(jnp.float32)
        return (
            resid_own.astype(jnp.float32) + streams_own[:, :, 1].astype(jnp.float32) * conv_out
        ).astype(jnp.bfloat16)

    def no_hyena(operand):
        return jnp.zeros_like(resid_own)

    hidden = lax.cond(section_index == 0, run_hyena, no_hyena, 0)
    attend = hidden.reshape(batch_count, tok_rows, local_heads, 2, HD)[:, :, :, 0].reshape(
        batch_count, tok_rows, attend_width
    )
    arrived = from_behind(attend, "pipe", 1)
    contig_ends = jnp.cumsum(contig_lengths, axis=1)
    reach_span = min(4, lax.axis_size("seq") // 2)
    pieces = [arrived]
    for distance in range(1, reach_span + 1):
        pieces.insert(0, from_behind(arrived, "seq", distance))
    key_source = jnp.concatenate(pieces, axis=1)
    key_rows = (reach_span + 1) * tok_rows

    def run_attention(operand):
        query_pos = seq_index * tok_rows + jnp.arange(tok_rows, dtype=jnp.int32)
        key_pos = (seq_index - reach_span) * tok_rows + jnp.arange(key_rows, dtype=jnp.int32)
        same = (
            segment_of(contig_ends, query_pos)[:, :, None]
            == segment_of(contig_ends, key_pos)[:, None, :]
        )
        causal = (key_pos[None, None, :] <= query_pos[None, :, None]) & (
            key_pos[None, None, :] >= 0
        )
        visible = same & causal
        queries = (
            (arrived.astype(jnp.float32) * q_gain)
            .astype(jnp.bfloat16)
            .reshape(batch_count, tok_rows, local_heads, HD)
        )
        keys = (
            (key_source.astype(jnp.float32) * k_gain)
            .astype(jnp.bfloat16)
            .reshape(batch_count, key_rows, local_heads, HD)
        )
        values = key_source.reshape(batch_count, key_rows, local_heads, HD)

        def one_batch(items):
            query_part, key_part, value_part, visible_part = items
            scores = (
                jnp.einsum("thd,shd->hts", query_part, key_part, preferred_element_type=jnp.float32)
                / HD
            )
            scores = jnp.where(visible_part[None], scores, NEG_FILL)
            top = jnp.max(scores, axis=-1, keepdims=True)
            weights = jnp.where(visible_part[None], jnp.exp(scores - top), 0.0)
            total = jnp.sum(weights, axis=-1)
            mixed = jnp.einsum(
                "hts,shd->thd",
                weights.astype(jnp.bfloat16),
                value_part,
                preferred_element_type=jnp.float32,
            )
            mixed = mixed / jnp.transpose(total)[..., None]
            return mixed.astype(jnp.bfloat16).reshape(tok_rows, attend_width)

        return lax.map(one_batch, (queries, keys, values, visible))

    def no_attention(operand):
        return jnp.zeros_like(arrived)

    mixed = lax.cond(section_index == 1, run_attention, no_attention, 0)
    all_heads = lax.all_gather(mixed, "tensor", axis=2, tiled=True)
    flattened = all_heads.reshape(batch_count * tok_rows, all_heads.shape[2])
    projected = jnp.dot(
        flattened,
        lax.all_gather(out_weight, "seq", axis=0, tiled=True),
        preferred_element_type=jnp.float32,
    )
    attn_out = projected.astype(jnp.bfloat16).reshape(batch_count, tok_rows, out_weight.shape[1])
    output = jnp.where(section_index == 0, hidden, attn_out)
    return output[None]


def landed(ref, sem):
    pltpu.make_async_copy(ref, ref, sem).wait()


def attention_kernel(
    n_seq, n_tensor, rows, streams_ref, resid_ref, filt_ref, gains_ref, begin_ref, weight_ref, out_ref,
    streams, resid, tail, tail_gated, prev, extended, attend,
    tokens, gains, queries, keys, own_mixed, mixed, weight, partial,
    send_a, recv_a, send_b, recv_b, send_y, recv_y,
    stream_sem, resid_sem, tail_sem, prev_send, prev_recv, hop_send, hop_recv,
    tok_send, tok_recv, gain_send, gain_recv, weight_sem, mix_send, mix_recv, mix_local,
    a_send, a_recv, b_send, b_recv, y_send, y_recv,
):
    pipe, seq, tensor = (lax.axis_index(name) for name in ("pipe", "seq", "tensor"))
    piece = tokens.shape[1]
    half = seq // 2
    inner = seq + half * (3 - 2 * seq)
    me = (pipe * n_seq + seq) * n_tensor + tensor
    world = 2 * n_seq * n_tensor
    barrier = pltpu.get_barrier_semaphore()

    fetch = pltpu.make_async_copy(weight_ref, weight, weight_sem)
    fetch_tail = pltpu.make_async_copy(streams_ref.at[:, :, pl.ds(rows - HALO, HALO)], tail, tail_sem)

    def fetch_stream(batch):
        return pltpu.make_async_copy(streams_ref.at[batch], streams.at[batch], stream_sem.at[batch])

    def fetch_resid(batch):
        return pltpu.make_async_copy(resid_ref.at[batch], resid.at[batch], resid_sem.at[batch])

    @pl.when(pipe == 0)
    def _():
        fetch_tail.start()
        for batch in (1, 0):
            fetch_stream(batch).start()
            fetch_resid(batch).start()

    fetch.start()

    def greet(step, carry):
        other = lax.rem(me + step, world)
        device = (other // (n_seq * n_tensor), other // n_tensor % n_seq, other % n_tensor)
        pl.semaphore_signal(barrier, inc=1, device_id=device, device_id_type=MESH)
        return carry

    lax.fori_loop(1, world, greet, 0)

    @pl.when(pipe == 0)
    def _():
        fetch_tail.wait()
        tail_gated[...] = (
            tail[:, 0].astype(jnp.float32) * tail[:, 2].astype(jnp.float32)
        ).astype(jnp.bfloat16)

    pl.semaphore_wait(barrier, world - 1)

    def remote(source, target, send_sem, recv_sem, device):
        return pltpu.make_async_remote_copy(
            src_ref=source, dst_ref=target, send_sem=send_sem, recv_sem=recv_sem,
            device_id=device, device_id_type=MESH,
        )

    def to_head_rows(turn):
        here = tokens.at[pl.ds(pl.multiple_of(seq * rows, rows), rows)]
        device = (pipe, tensor, turn)
        is_self = (seq == tensor) & (turn == tensor)
        return is_self, (
            attend.at[pipe, turn], here, tok_send.at[turn], tok_recv.at[seq], device
        ), (gains_ref.at[turn], gains, gain_send.at[turn], gain_recv.at[0], device)

    def send_turn(turn):
        is_self, block, gain = to_head_rows(turn)

        @pl.when(jnp.logical_not(is_self))
        def _():
            remote(*block).start()

        @pl.when(jnp.logical_not(is_self) & (seq == 0))
        def _():
            remote(*gain).start()

        @pl.when(is_self)
        def _():
            pltpu.make_async_copy(block[0], block[1], block[3]).start()

        @pl.when(is_self & (seq == 0))
        def _():
            pltpu.make_async_copy(gain[0], gain[1], gain[3]).start()

    def wait_turn(turn, carry):
        is_self, block, gain = to_head_rows(turn)

        @pl.when(jnp.logical_not(is_self))
        def _():
            remote(*block).wait_send()

        @pl.when(jnp.logical_not(is_self) & (seq == 0))
        def _():
            remote(*gain).wait_send()

        return carry

    def hop(turn):
        return remote(
            attend.at[1, turn], attend.at[1, turn], hop_send.at[turn], hop_recv.at[turn],
            (1, seq, tensor),
        )

    def send_prev():
        return remote(tail_gated, prev, prev_send, prev_recv, (0, seq + 1, tensor))

    def hyena(batch, column, keep):
        lanes = pl.ds(pl.multiple_of(column, HD), HD)
        taps = [filt_ref[j : j + 1, lanes].astype(jnp.float32) for j in range(filt_ref.shape[0])]
        step = 64
        for row in range(0, rows, step):
            conv = jnp.zeros((step, HD), jnp.float32)
            for j, tap in enumerate(taps):
                conv = conv + tap * extended[batch, pl.ds(HALO + row - j, step), lanes]
            own = pl.ds(row, step)
            out_gate = streams[batch, 1, own, lanes].astype(jnp.float32)
            hidden = resid[batch, own, lanes].astype(jnp.float32) + out_gate * conv
            hidden = hidden.astype(jnp.bfloat16)
            out_ref[batch, own, lanes] = hidden
            keep(own, hidden)

    @pl.when(pipe == 0)
    def _():
        @pl.when(seq < n_seq - 1)
        def _():
            send_prev().start()

        for batch in (1, 0):
            fetch_stream(batch).wait()

            def gate(strip, carry):
                own = pl.ds(pl.multiple_of(strip * 16, 16), 16)
                here = pl.ds(pl.multiple_of(HALO + strip * 16, 16), 16)
                gated = streams[batch, 0, own].astype(jnp.float32) * streams[batch, 2, own].astype(jnp.float32)
                extended[batch, here] = gated.astype(jnp.bfloat16).astype(jnp.float32)
                return carry

            lax.fori_loop(0, rows // 16, gate, 0)

        @pl.when(seq == 0)
        def _():
            extended[:, :HALO] = jnp.zeros((2, HALO, extended.shape[2]), jnp.float32)

        @pl.when(seq > 0)
        def _():
            landed(prev, prev_recv)
            extended[:, :HALO] = prev[...].astype(jnp.float32)

        for batch in (1, 0):
            fetch_resid(batch).wait()

        def attended(turn, carry):
            batch, other = 1 - turn // n_tensor, turn % n_tensor
            for head in range(piece // HD):

                def keep(own, hidden):
                    attend[batch, other, own, head * HD : (head + 1) * HD] = hidden

                hyena(batch, (other * (piece // HD) + head) * 2 * HD, keep)

            @pl.when(batch == 1)
            def _():
                hop(other).start()

            @pl.when(batch == 0)
            def _():
                send_turn(other)

            return carry

        lax.fori_loop(0, 2 * n_tensor, attended, 0)

    def unattended(turn, carry):
        batch, other = 1 - turn // n_tensor, turn % n_tensor
        for head in range(piece // HD):
            hyena(batch, (other * (piece // HD) + head) * 2 * HD + HD, lambda own, hidden: None)
        return carry

    @pl.when(pipe == 1)
    def _():
        def pass_on(turn, carry):
            landed(attend.at[1, turn], hop_recv.at[turn])
            send_turn(turn)
            return carry

        lax.fori_loop(0, n_tensor, pass_on, 0)

    landed(gains, gain_recv.at[0])
    for source in range(n_seq):
        here = slice(source * rows, (source + 1) * rows)
        landed(tokens.at[here], tok_recv.at[source])
        block = tokens[here].astype(jnp.float32)
        queries[here] = (block * gains[0:1]).astype(jnp.bfloat16)
        keys[here] = (block * gains[1:2]).astype(jnp.bfloat16)

    window = min(3, n_seq) * rows
    mine = pl.ds(pl.multiple_of(tensor * piece, piece), piece)

    def chunk_of(step):
        order = (3 - step) + (step // 2) * (inner * (2 * step - 5))
        return order + half * (3 - 2 * order)

    def mix_copy(step, stride):
        return remote(
            own_mixed.at[step], mixed.at[step, :, mine], mix_send.at[step, stride - 1],
            mix_recv.at[step, tensor], (pipe, seq, lax.rem(tensor + stride, n_tensor)),
        )

    def attention(step):
        chunk = chunk_of(step)
        first = pl.multiple_of(chunk * rows, rows)
        low = pl.multiple_of((chunk // 3) * rows, rows)
        position = first + lax.broadcasted_iota(jnp.int32, (rows, window), 0)
        key_position = low + lax.broadcasted_iota(jnp.int32, (rows, window), 1)
        visible = (key_position >= begin_ref[pl.ds(first, rows)]) & (key_position <= position)
        for head in range(piece // HD):
            lanes = slice(head * HD, (head + 1) * HD)
            scores = lax.dot_general(
                queries[pl.ds(first, rows), lanes], keys[pl.ds(low, window), lanes],
                (((1,), (1,)), ((), ())), preferred_element_type=jnp.float32,
            ) * (1.0 / HD)
            scores = jnp.where(visible, scores, NEG_FILL)
            weights = jnp.exp(scores - jnp.max(scores, axis=1, keepdims=True))
            total = jnp.sum(weights, axis=1, keepdims=True)
            result = jnp.dot(
                weights.astype(jnp.bfloat16), tokens[pl.ds(low, window), lanes],
                preferred_element_type=jnp.float32,
            )
            own_mixed[step, :, lanes] = (result / total).astype(jnp.bfloat16)
        pltpu.make_async_copy(own_mixed.at[step], mixed.at[step, :, mine], mix_local.at[step]).start()
        for stride in range(1, n_tensor):
            mix_copy(step, stride).start()

    def inward(step, part):
        return remote(
            send_a.at[step, part], recv_a.at[step, part], a_send.at[step, part],
            a_recv.at[step, part], (pipe, 1 + half, tensor),
        )

    def project(step):
        pltpu.make_async_copy(own_mixed.at[step], mixed.at[step, :, mine], mix_local.at[step]).wait()
        for stride in range(1, n_tensor):
            source = lax.rem(tensor + stride, n_tensor)
            lanes = pl.ds(pl.multiple_of(source * piece, piece), piece)
            landed(mixed.at[step, :, lanes], mix_recv.at[step, source])
        width = partial.shape[3]
        for part in range(PARTS):
            value = jnp.dot(
                mixed[step], weight[:, part * width : (part + 1) * width],
                preferred_element_type=jnp.float32,
            )
            partial[step, part] = value

            @pl.when((inner == 0) & (step < 3))
            def _():
                send_a[step, part] = value.astype(jnp.bfloat16)
                inward(step, part).start()

    def turn(step, carry):
        @pl.when(step < 4)
        def _():
            attention(step)

        @pl.when(step == 1)
        def _():
            fetch.wait()

        @pl.when(step > 0)
        def _():
            project(step - 1)

        return carry

    lax.fori_loop(0, 5, turn, 0)

    @pl.when(pipe == 0)
    def _():
        lax.fori_loop(0, 2 * n_tensor, unattended, 0)

    def across(step, part):
        return remote(
            send_a.at[step, part], recv_b.at[step, part], b_send.at[step, part],
            b_recv.at[step, part], (pipe, 3 - seq, tensor),
        )

    def outward(part):
        return remote(
            send_b.at[part], recv_b.at[0, part], b_send.at[2, part],
            b_recv.at[0, part], (pipe, 3 * half, tensor),
        )

    def home(part):
        return remote(
            send_y.at[part], recv_y.at[part], y_send.at[part], y_recv.at[part], (1, seq, tensor)
        )

    def finish(part, value):
        width = value.shape[1]

        @pl.when(pipe == 0)
        def _():
            send_y[part] = value.astype(jnp.bfloat16)
            home(part).start()

        @pl.when(pipe == 1)
        def _():
            out_ref[1, :, part * width : (part + 1) * width] = value.astype(jnp.bfloat16)

    def forward(step, part):
        landed(recv_a.at[step, part], a_recv.at[step, part])
        send_a[step, part] = (partial[step, part] + recv_a[step, part].astype(jnp.float32)).astype(jnp.bfloat16)
        across(step, part).start()

    def relay(part):
        landed(recv_b.at[0, part], b_recv.at[0, part])
        send_b[part] = (partial[2, part] + recv_b[0, part].astype(jnp.float32)).astype(jnp.bfloat16)
        outward(part).start()

    @pl.when(inner == 1)
    def _():
        for part in range(PARTS):
            forward(0, part)
            if part > 0:
                relay(part - 1)
        relay(PARTS - 1)
        for part in range(PARTS):
            forward(1, part)
        for part in range(PARTS):
            landed(recv_a.at[2, part], a_recv.at[2, part])
            landed(recv_b.at[1, part], b_recv.at[1, part])
            finish(part, partial[3, part] + recv_a[2, part].astype(jnp.float32) + recv_b[1, part].astype(jnp.float32))
        for part in range(PARTS):
            across(0, part).wait_send()
            across(1, part).wait_send()
            outward(part).wait_send()

    @pl.when(inner == 0)
    def _():
        for part in range(PARTS):
            landed(recv_b.at[0, part], b_recv.at[0, part])
            finish(part, partial[3, part] + recv_b[0, part].astype(jnp.float32))
        for step in range(3):
            for part in range(PARTS):
                inward(step, part).wait_send()

    @pl.when(pipe == 1)
    def _():
        width = recv_y.shape[2]
        for part in range(PARTS):
            landed(recv_y.at[part], y_recv.at[part])
            out_ref[0, :, part * width : (part + 1) * width] = recv_y[part]

    @pl.when(pipe == 0)
    def _():
        for part in range(PARTS):
            home(part).wait_send()
        for step in range(n_tensor):
            hop(step).wait_send()

        @pl.when(seq < n_seq - 1)
        def _():
            send_prev().wait_send()

    lax.fori_loop(0, n_tensor, wait_turn, 0)
    for step in range(4):
        for stride in range(1, n_tensor):
            mix_copy(step, stride).wait_send()


def run_sections(streams, resid, filt, gains, begins, weight, n_seq, n_tensor):
    batch, rows = resid.shape[:2]
    piece = gains.shape[2]
    depth, width = weight.shape
    length = n_seq * rows
    part = width // PARTS
    bf16, f32 = jnp.bfloat16, jnp.float32
    dma = pltpu.SemaphoreType.DMA
    anywhere, vmem = pl.BlockSpec(memory_space=pl.ANY), pl.BlockSpec(memory_space=pltpu.VMEM)
    return pl.pallas_call(
        functools.partial(attention_kernel, n_seq, n_tensor, rows),
        in_specs=[anywhere, anywhere, vmem, anywhere, vmem, anywhere],
        out_specs=vmem,
        out_shape=jax.ShapeDtypeStruct((batch, rows, width), bf16),
        scratch_shapes=[
            pltpu.VMEM(streams.shape, bf16),
            pltpu.VMEM(resid.shape, bf16),
            pltpu.VMEM((batch, 3, HALO, width), bf16),
            pltpu.VMEM((batch, HALO, width), bf16),
            pltpu.VMEM((batch, HALO, width), bf16),
            pltpu.VMEM((batch, HALO + rows, width), f32),
            pltpu.VMEM((batch, n_tensor, rows, piece), bf16),
            pltpu.VMEM((length, piece), bf16),
            pltpu.VMEM(gains.shape[1:], f32),
            pltpu.VMEM((length, piece), bf16),
            pltpu.VMEM((length, piece), bf16),
            pltpu.VMEM((4, rows, piece), bf16),
            pltpu.VMEM((4, rows, depth), bf16),
            pltpu.VMEM((depth, width), bf16),
            pltpu.VMEM((4, PARTS, rows, part), f32),
            pltpu.VMEM((3, PARTS, rows, part), bf16),
            pltpu.VMEM((3, PARTS, rows, part), bf16),
            pltpu.VMEM((PARTS, rows, part), bf16),
            pltpu.VMEM((2, PARTS, rows, part), bf16),
            pltpu.VMEM((PARTS, rows, part), bf16),
            pltpu.VMEM((PARTS, rows, part), bf16),
            dma((batch,)), dma((batch,)), dma, dma, dma,
            dma((n_tensor,)), dma((n_tensor,)),
            dma((n_tensor,)), dma((n_seq,)), dma((n_tensor,)), dma((1,)), dma,
            dma((4, n_tensor - 1)), dma((4, n_tensor)), dma((4,)),
            dma((3, PARTS)), dma((3, PARTS)), dma((3, PARTS)), dma((2, PARTS)),
            dma((PARTS,)), dma((PARTS,)),
        ],
        compiler_params=pltpu.CompilerParams(
            collective_id=0, has_side_effects=True, vmem_limit_bytes=56 << 20
        ),
        name="sections",
    )(streams, resid, filt, gains, begins, weight)


def sums_travel(resid, streams, filt, q_gain, k_gain, out_weight, contig_lengths):
    n_seq, n_tensor = lax.axis_size("seq"), lax.axis_size("tensor")
    section = lax.axis_index("pipe")
    rows = resid.shape[2]
    gains = jnp.stack([q_gain.reshape(n_tensor, -1), k_gain.reshape(n_tensor, -1)], axis=1)
    gains = jnp.pad(gains, ((0, 0), (0, 6), (0, 0)))
    ends = jnp.cumsum(jnp.where(section == 0, contig_lengths[0], contig_lengths[1]))
    position = jnp.arange(n_seq * rows, dtype=jnp.int32)
    begins = jnp.max(jnp.where(ends[None] <= position[:, None], ends[None], 0), axis=1, keepdims=True)
    return run_sections(
        jnp.transpose(streams[0], (0, 2, 1, 3)), resid[0], filt, gains, begins.astype(jnp.int32),
        out_weight, n_seq, n_tensor,
    )[None]


def solution(mesh):
    few = mesh.shape["seq"] == 4 and mesh.shape["tensor"] == 4 and mesh.shape["pipe"] == 2
    per_device = sums_travel if few else weights_travel
    placed = (
        P("pipe", None, "seq", "tensor"),
        P("pipe", None, "seq", None, "tensor"),
        P(None, "tensor"),
        P("tensor"),
        P("tensor"),
        P("seq", "tensor"),
        P(),
    )
    return jax.shard_map(
        per_device,
        mesh=mesh,
        in_specs=placed,
        out_specs=P("pipe", None, "seq", "tensor"),
        check_vma=False,
    )
```

```python
import functools

import jax
import jax.numpy as jnp
from jax import lax
from jax.experimental import pallas as pl
from jax.experimental.pallas import tpu as pltpu
from jax.sharding import PartitionSpec as P

HD = 128
MESH = pl.DeviceIdType.MESH
HALO = 16
PARTS = 8


NEG_FILL = -1e30


def from_behind(value, axis, steps):
    count = lax.axis_size(axis)
    first, last = (max(0, -steps), min(count, count - steps))
    return lax.ppermute(value, axis, [(source, source + steps) for source in range(first, last)])


def segment_of(contig_ends, positions):
    return jnp.sum((contig_ends[:, None, :] <= positions[None, :, None]).astype(jnp.int32), axis=2)


def weights_travel(resid, streams, filt, q_gain, k_gain, out_weight, contig_lengths):
    resid_own = resid[0]
    streams_own = streams[0]
    tap_count = filt.shape[0]
    batch_count = resid_own.shape[0]
    tok_rows = resid_own.shape[1]
    local_heads = q_gain.shape[0] // HD
    attend_width = local_heads * HD
    section_index = lax.axis_index("pipe")
    seq_index = lax.axis_index("seq")
    gated = (
        streams_own[:, :, 0].astype(jnp.float32) * streams_own[:, :, 2].astype(jnp.float32)
    ).astype(jnp.bfloat16)
    prev_rows = from_behind(gated[:, tok_rows - (tap_count - 1) :], "seq", 1)

    def run_hyena(operand):
        extended = jnp.concatenate([prev_rows, gated], axis=1)
        conv_out = jnp.zeros(resid_own.shape, jnp.float32)
        for offset in range(tap_count):
            begin = tap_count - 1 - offset
            conv_out = conv_out + filt[offset].astype(jnp.float32) * extended[
                :, begin : begin + tok_rows
            ].astype(jnp.float32)
        return (
            resid_own.astype(jnp.float32) + streams_own[:, :, 1].astype(jnp.float32) * conv_out
        ).astype(jnp.bfloat16)

    def no_hyena(operand):
        return jnp.zeros_like(resid_own)

    hidden = lax.cond(section_index == 0, run_hyena, no_hyena, 0)
    attend = hidden.reshape(batch_count, tok_rows, local_heads, 2, HD)[:, :, :, 0].reshape(
        batch_count, tok_rows, attend_width
    )
    arrived = from_behind(attend, "pipe", 1)
    contig_ends = jnp.cumsum(contig_lengths, axis=1)
    reach_span = min(4, lax.axis_size("seq") // 2)
    pieces = [arrived]
    for distance in range(1, reach_span + 1):
        pieces.insert(0, from_behind(arrived, "seq", distance))
    key_source = jnp.concatenate(pieces, axis=1)
    key_rows = (reach_span + 1) * tok_rows

    def run_attention(operand):
        query_pos = seq_index * tok_rows + jnp.arange(tok_rows, dtype=jnp.int32)
        key_pos = (seq_index - reach_span) * tok_rows + jnp.arange(key_rows, dtype=jnp.int32)
        same = (
            segment_of(contig_ends, query_pos)[:, :, None]
            == segment_of(contig_ends, key_pos)[:, None, :]
        )
        causal = (key_pos[None, None, :] <= query_pos[None, :, None]) & (
            key_pos[None, None, :] >= 0
        )
        visible = same & causal
        queries = (
            (arrived.astype(jnp.float32) * q_gain)
            .astype(jnp.bfloat16)
            .reshape(batch_count, tok_rows, local_heads, HD)
        )
        keys = (
            (key_source.astype(jnp.float32) * k_gain)
            .astype(jnp.bfloat16)
            .reshape(batch_count, key_rows, local_heads, HD)
        )
        values = key_source.reshape(batch_count, key_rows, local_heads, HD)

        def one_batch(items):
            query_part, key_part, value_part, visible_part = items
            scores = (
                jnp.einsum("thd,shd->hts", query_part, key_part, preferred_element_type=jnp.float32)
                / HD
            )
            scores = jnp.where(visible_part[None], scores, NEG_FILL)
            top = jnp.max(scores, axis=-1, keepdims=True)
            weights = jnp.where(visible_part[None], jnp.exp(scores - top), 0.0)
            total = jnp.sum(weights, axis=-1)
            mixed = jnp.einsum(
                "hts,shd->thd",
                weights.astype(jnp.bfloat16),
                value_part,
                preferred_element_type=jnp.float32,
            )
            mixed = mixed / jnp.transpose(total)[..., None]
            return mixed.astype(jnp.bfloat16).reshape(tok_rows, attend_width)

        return lax.map(one_batch, (queries, keys, values, visible))

    def no_attention(operand):
        return jnp.zeros_like(arrived)

    mixed = lax.cond(section_index == 1, run_attention, no_attention, 0)
    all_heads = lax.all_gather(mixed, "tensor", axis=2, tiled=True)
    flattened = all_heads.reshape(batch_count * tok_rows, all_heads.shape[2])
    projected = jnp.dot(
        flattened,
        lax.all_gather(out_weight, "seq", axis=0, tiled=True),
        preferred_element_type=jnp.float32,
    )
    attn_out = projected.astype(jnp.bfloat16).reshape(batch_count, tok_rows, out_weight.shape[1])
    output = jnp.where(section_index == 0, hidden, attn_out)
    return output[None]


def landed(ref, sem):
    pltpu.make_async_copy(ref, ref, sem).wait()


def attention_kernel(
    n_seq, n_tensor, rows, streams_ref, resid_ref, filt_ref, gains_ref, lengths_ref, weight_ref, out_ref,
    streams, resid, tail, tail_gated, prev, extended, attend,
    tokens, gains, queries, keys, own_mixed, mixed, weight, partial,
    send_a, recv_a, send_b, recv_b, send_y, recv_y,
    stream_sem, resid_sem, tail_sem, prev_send, prev_recv, hop_send, hop_recv,
    tok_send, tok_recv, gain_send, gain_recv, weight_sem, mix_send, mix_recv, mix_local,
    a_send, a_recv, b_send, b_recv, y_send, y_recv,
):
    pipe, seq, tensor = (lax.axis_index(name) for name in ("pipe", "seq", "tensor"))
    piece = tokens.shape[1]
    half = seq // 2
    inner = seq + half * (3 - 2 * seq)
    me = (pipe * n_seq + seq) * n_tensor + tensor
    world = 2 * n_seq * n_tensor
    barrier = pltpu.get_barrier_semaphore()

    fetch = pltpu.make_async_copy(weight_ref, weight, weight_sem)
    fetch_tail = pltpu.make_async_copy(streams_ref.at[:, :, pl.ds(rows - HALO, HALO)], tail, tail_sem)

    def fetch_stream(batch):
        return pltpu.make_async_copy(streams_ref.at[batch], streams.at[batch], stream_sem.at[batch])

    def fetch_resid(batch):
        return pltpu.make_async_copy(resid_ref.at[batch], resid.at[batch], resid_sem.at[batch])

    @pl.when(pipe == 0)
    def _():
        fetch_tail.start()
        for batch in (1, 0):
            fetch_stream(batch).start()
            fetch_resid(batch).start()

    fetch.start()

    def greet(step, carry):
        other = lax.rem(me + step, world)
        device = (other // (n_seq * n_tensor), other // n_tensor % n_seq, other % n_tensor)
        pl.semaphore_signal(barrier, inc=1, device_id=device, device_id_type=MESH)
        return carry

    lax.fori_loop(1, world, greet, 0)

    @pl.when(pipe == 0)
    def _():
        fetch_tail.wait()
        tail_gated[...] = (
            tail[:, 0].astype(jnp.float32) * tail[:, 2].astype(jnp.float32)
        ).astype(jnp.bfloat16)

    pl.semaphore_wait(barrier, world - 1)

    def remote(source, target, send_sem, recv_sem, device):
        return pltpu.make_async_remote_copy(
            src_ref=source, dst_ref=target, send_sem=send_sem, recv_sem=recv_sem,
            device_id=device, device_id_type=MESH,
        )

    def to_head_rows(turn):
        here = tokens.at[pl.ds(pl.multiple_of(seq * rows, rows), rows)]
        device = (pipe, tensor, turn)
        is_self = (seq == tensor) & (turn == tensor)
        return is_self, (
            attend.at[pipe, turn], here, tok_send.at[turn], tok_recv.at[seq], device
        ), (gains_ref.at[turn], gains, gain_send.at[turn], gain_recv.at[0], device)

    def send_turn(turn):
        is_self, block, gain = to_head_rows(turn)

        @pl.when(jnp.logical_not(is_self))
        def _():
            remote(*block).start()

        @pl.when(jnp.logical_not(is_self) & (seq == 0))
        def _():
            remote(*gain).start()

        @pl.when(is_self)
        def _():
            pltpu.make_async_copy(block[0], block[1], block[3]).start()

        @pl.when(is_self & (seq == 0))
        def _():
            pltpu.make_async_copy(gain[0], gain[1], gain[3]).start()

    def wait_turn(turn, carry):
        is_self, block, gain = to_head_rows(turn)

        @pl.when(jnp.logical_not(is_self))
        def _():
            remote(*block).wait_send()

        @pl.when(jnp.logical_not(is_self) & (seq == 0))
        def _():
            remote(*gain).wait_send()

        return carry

    def hop(turn):
        return remote(
            attend.at[1, turn], attend.at[1, turn], hop_send.at[turn], hop_recv.at[turn],
            (1, seq, tensor),
        )

    def send_prev():
        return remote(tail_gated, prev, prev_send, prev_recv, (0, seq + 1, tensor))

    def hyena(batch, column, keep):
        lanes = pl.ds(pl.multiple_of(column, HD), HD)
        taps = [filt_ref[j : j + 1, lanes].astype(jnp.float32) for j in range(filt_ref.shape[0])]
        step = 64
        for row in range(0, rows, step):
            conv = jnp.zeros((step, HD), jnp.float32)
            for j, tap in enumerate(taps):
                conv = conv + tap * extended[batch, pl.ds(HALO + row - j, step), lanes]
            own = pl.ds(row, step)
            out_gate = streams[batch, 1, own, lanes].astype(jnp.float32)
            hidden = resid[batch, own, lanes].astype(jnp.float32) + out_gate * conv
            hidden = hidden.astype(jnp.bfloat16)
            out_ref[batch, own, lanes] = hidden
            keep(own, hidden)

    @pl.when(pipe == 0)
    def _():
        @pl.when(seq < n_seq - 1)
        def _():
            send_prev().start()

        for batch in (1, 0):
            fetch_stream(batch).wait()

            def gate(strip, carry):
                own = pl.ds(pl.multiple_of(strip * 16, 16), 16)
                here = pl.ds(pl.multiple_of(HALO + strip * 16, 16), 16)
                gated = streams[batch, 0, own].astype(jnp.float32) * streams[batch, 2, own].astype(jnp.float32)
                extended[batch, here] = gated.astype(jnp.bfloat16).astype(jnp.float32)
                return carry

            lax.fori_loop(0, rows // 16, gate, 0)

        @pl.when(seq == 0)
        def _():
            extended[:, :HALO] = jnp.zeros((2, HALO, extended.shape[2]), jnp.float32)

        @pl.when(seq > 0)
        def _():
            landed(prev, prev_recv)
            extended[:, :HALO] = prev[...].astype(jnp.float32)

        for batch in (1, 0):
            fetch_resid(batch).wait()

        def attended(turn, carry):
            batch, other = 1 - turn // n_tensor, turn % n_tensor
            for head in range(piece // HD):

                def keep(own, hidden):
                    attend[batch, other, own, head * HD : (head + 1) * HD] = hidden

                hyena(batch, (other * (piece // HD) + head) * 2 * HD, keep)

            @pl.when(batch == 1)
            def _():
                hop(other).start()

            @pl.when(batch == 0)
            def _():
                send_turn(other)

            return carry

        lax.fori_loop(0, 2 * n_tensor, attended, 0)

    def unattended(turn, carry):
        batch, other = 1 - turn // n_tensor, turn % n_tensor
        for head in range(piece // HD):
            hyena(batch, (other * (piece // HD) + head) * 2 * HD + HD, lambda own, hidden: None)
        return carry

    @pl.when(pipe == 1)
    def _():
        def pass_on(turn, carry):
            landed(attend.at[1, turn], hop_recv.at[turn])
            send_turn(turn)
            return carry

        lax.fori_loop(0, n_tensor, pass_on, 0)

    landed(gains, gain_recv.at[0])
    for source in range(n_seq):
        here = slice(source * rows, (source + 1) * rows)
        landed(tokens.at[here], tok_recv.at[source])
        block = tokens[here].astype(jnp.float32)
        queries[here] = (block * gains[0:1]).astype(jnp.bfloat16)
        keys[here] = (block * gains[1:2]).astype(jnp.bfloat16)

    window = min(3, n_seq) * rows
    mine = pl.ds(pl.multiple_of(tensor * piece, piece), piece)

    def chunk_of(step):
        order = (3 - step) + (step // 2) * (inner * (2 * step - 5))
        return order + half * (3 - 2 * order)

    def mix_copy(step, stride):
        return remote(
            own_mixed.at[step], mixed.at[step, :, mine], mix_send.at[step, stride - 1],
            mix_recv.at[step, tensor], (pipe, seq, lax.rem(tensor + stride, n_tensor)),
        )

    def attention(step):
        chunk = chunk_of(step)
        first = pl.multiple_of(chunk * rows, rows)
        low = pl.multiple_of((chunk // 3) * rows, rows)
        position = first + lax.broadcasted_iota(jnp.int32, (rows, window), 0)
        key_position = low + lax.broadcasted_iota(jnp.int32, (rows, window), 1)
        token = first + lax.broadcasted_iota(jnp.int32, (rows, 1), 0)
        begin, end = jnp.zeros((rows, 1), jnp.int32), 0
        for contig in range(lengths_ref.shape[1]):
            end = end + lengths_ref[pipe, contig]
            begin = jnp.where(token >= end, end, begin)
        visible = (key_position >= begin) & (key_position <= position)
        for head in range(piece // HD):
            lanes = slice(head * HD, (head + 1) * HD)
            scores = lax.dot_general(
                queries[pl.ds(first, rows), lanes], keys[pl.ds(low, window), lanes],
                (((1,), (1,)), ((), ())), preferred_element_type=jnp.float32,
            ) * (1.0 / HD)
            scores = jnp.where(visible, scores, NEG_FILL)
            weights = jnp.exp(scores - jnp.max(scores, axis=1, keepdims=True))
            total = jnp.sum(weights, axis=1, keepdims=True)
            result = jnp.dot(
                weights.astype(jnp.bfloat16), tokens[pl.ds(low, window), lanes],
                preferred_element_type=jnp.float32,
            )
            own_mixed[step, :, lanes] = (result / total).astype(jnp.bfloat16)
        pltpu.make_async_copy(own_mixed.at[step], mixed.at[step, :, mine], mix_local.at[step]).start()
        for stride in range(1, n_tensor):
            mix_copy(step, stride).start()

    def inward(step, part):
        return remote(
            send_a.at[step, part], recv_a.at[step, part], a_send.at[step, part],
            a_recv.at[step, part], (pipe, 1 + half, tensor),
        )

    def project(step):
        pltpu.make_async_copy(own_mixed.at[step], mixed.at[step, :, mine], mix_local.at[step]).wait()
        for stride in range(1, n_tensor):
            source = lax.rem(tensor + stride, n_tensor)
            lanes = pl.ds(pl.multiple_of(source * piece, piece), piece)
            landed(mixed.at[step, :, lanes], mix_recv.at[step, source])
        width = partial.shape[3]
        for part in range(PARTS):
            value = jnp.dot(
                mixed[step], weight[:, part * width : (part + 1) * width],
                preferred_element_type=jnp.float32,
            )
            partial[step, part] = value

            @pl.when((inner == 0) & (step < 3))
            def _():
                send_a[step, part] = value.astype(jnp.bfloat16)
                inward(step, part).start()

    def turn(step, carry):
        @pl.when(step < 4)
        def _():
            attention(step)

        @pl.when(step == 1)
        def _():
            fetch.wait()

        @pl.when(step > 0)
        def _():
            project(step - 1)

        return carry

    lax.fori_loop(0, 5, turn, 0)

    @pl.when(pipe == 0)
    def _():
        lax.fori_loop(0, 2 * n_tensor, unattended, 0)

    def across(step, part):
        return remote(
            send_a.at[step, part], recv_b.at[step, part], b_send.at[step, part],
            b_recv.at[step, part], (pipe, 3 - seq, tensor),
        )

    def outward(part):
        return remote(
            send_b.at[part], recv_b.at[0, part], b_send.at[2, part],
            b_recv.at[0, part], (pipe, 3 * half, tensor),
        )

    def home(part):
        return remote(
            send_y.at[part], recv_y.at[part], y_send.at[part], y_recv.at[part], (1, seq, tensor)
        )

    def finish(part, value):
        width = value.shape[1]

        @pl.when(pipe == 0)
        def _():
            send_y[part] = value.astype(jnp.bfloat16)
            home(part).start()

        @pl.when(pipe == 1)
        def _():
            out_ref[1, :, part * width : (part + 1) * width] = value.astype(jnp.bfloat16)

    def forward(step, part):
        landed(recv_a.at[step, part], a_recv.at[step, part])
        send_a[step, part] = (partial[step, part] + recv_a[step, part].astype(jnp.float32)).astype(jnp.bfloat16)
        across(step, part).start()

    def relay(part):
        landed(recv_b.at[0, part], b_recv.at[0, part])
        send_b[part] = (partial[2, part] + recv_b[0, part].astype(jnp.float32)).astype(jnp.bfloat16)
        outward(part).start()

    @pl.when(inner == 1)
    def _():
        for part in range(PARTS):
            forward(0, part)
            if part > 0:
                relay(part - 1)
        relay(PARTS - 1)
        for part in range(PARTS):
            forward(1, part)
        for part in range(PARTS):
            landed(recv_a.at[2, part], a_recv.at[2, part])
            landed(recv_b.at[1, part], b_recv.at[1, part])
            finish(part, partial[3, part] + recv_a[2, part].astype(jnp.float32) + recv_b[1, part].astype(jnp.float32))
        for part in range(PARTS):
            across(0, part).wait_send()
            across(1, part).wait_send()
            outward(part).wait_send()

    @pl.when(inner == 0)
    def _():
        for part in range(PARTS):
            landed(recv_b.at[0, part], b_recv.at[0, part])
            finish(part, partial[3, part] + recv_b[0, part].astype(jnp.float32))
        for step in range(3):
            for part in range(PARTS):
                inward(step, part).wait_send()

    @pl.when(pipe == 1)
    def _():
        width = recv_y.shape[2]
        for part in range(PARTS):
            landed(recv_y.at[part], y_recv.at[part])
            out_ref[0, :, part * width : (part + 1) * width] = recv_y[part]

    @pl.when(pipe == 0)
    def _():
        for part in range(PARTS):
            home(part).wait_send()
        for step in range(n_tensor):
            hop(step).wait_send()

        @pl.when(seq < n_seq - 1)
        def _():
            send_prev().wait_send()

    lax.fori_loop(0, n_tensor, wait_turn, 0)
    for step in range(4):
        for stride in range(1, n_tensor):
            mix_copy(step, stride).wait_send()


def run_sections(streams, resid, filt, gains, lengths, weight, n_seq, n_tensor):
    batch, rows = resid.shape[:2]
    piece = gains.shape[2]
    depth, width = weight.shape
    length = n_seq * rows
    part = width // PARTS
    bf16, f32 = jnp.bfloat16, jnp.float32
    dma = pltpu.SemaphoreType.DMA
    anywhere, vmem = pl.BlockSpec(memory_space=pl.ANY), pl.BlockSpec(memory_space=pltpu.VMEM)
    return pl.pallas_call(
        functools.partial(attention_kernel, n_seq, n_tensor, rows),
        in_specs=[anywhere, anywhere, vmem, anywhere, pl.BlockSpec(memory_space=pltpu.SMEM), anywhere],
        out_specs=vmem,
        out_shape=jax.ShapeDtypeStruct((batch, rows, width), bf16),
        scratch_shapes=[
            pltpu.VMEM(streams.shape, bf16),
            pltpu.VMEM(resid.shape, bf16),
            pltpu.VMEM((batch, 3, HALO, width), bf16),
            pltpu.VMEM((batch, HALO, width), bf16),
            pltpu.VMEM((batch, HALO, width), bf16),
            pltpu.VMEM((batch, HALO + rows, width), f32),
            pltpu.VMEM((batch, n_tensor, rows, piece), bf16),
            pltpu.VMEM((length, piece), bf16),
            pltpu.VMEM(gains.shape[1:], f32),
            pltpu.VMEM((length, piece), bf16),
            pltpu.VMEM((length, piece), bf16),
            pltpu.VMEM((4, rows, piece), bf16),
            pltpu.VMEM((4, rows, depth), bf16),
            pltpu.VMEM((depth, width), bf16),
            pltpu.VMEM((4, PARTS, rows, part), f32),
            pltpu.VMEM((3, PARTS, rows, part), bf16),
            pltpu.VMEM((3, PARTS, rows, part), bf16),
            pltpu.VMEM((PARTS, rows, part), bf16),
            pltpu.VMEM((2, PARTS, rows, part), bf16),
            pltpu.VMEM((PARTS, rows, part), bf16),
            pltpu.VMEM((PARTS, rows, part), bf16),
            dma((batch,)), dma((batch,)), dma, dma, dma,
            dma((n_tensor,)), dma((n_tensor,)),
            dma((n_tensor,)), dma((n_seq,)), dma((n_tensor,)), dma((1,)), dma,
            dma((4, n_tensor - 1)), dma((4, n_tensor)), dma((4,)),
            dma((3, PARTS)), dma((3, PARTS)), dma((3, PARTS)), dma((2, PARTS)),
            dma((PARTS,)), dma((PARTS,)),
        ],
        compiler_params=pltpu.CompilerParams(
            collective_id=0, has_side_effects=True, vmem_limit_bytes=56 << 20
        ),
        name="sections",
    )(streams, resid, filt, gains, lengths, weight)


def sums_travel(resid, streams, filt, q_gain, k_gain, out_weight, contig_lengths):
    n_seq, n_tensor = lax.axis_size("seq"), lax.axis_size("tensor")
    gains = jnp.stack([q_gain.reshape(n_tensor, -1), k_gain.reshape(n_tensor, -1)], axis=1)
    gains = jnp.pad(gains, ((0, 0), (0, 6), (0, 0)))
    return run_sections(
        jnp.transpose(streams[0], (0, 2, 1, 3)), resid[0], filt, gains, contig_lengths,
        out_weight, n_seq, n_tensor,
    )[None]


def solution(mesh):
    few = mesh.shape["seq"] == 4 and mesh.shape["tensor"] == 4 and mesh.shape["pipe"] == 2
    per_device = sums_travel if few else weights_travel
    placed = (
        P("pipe", None, "seq", "tensor"),
        P("pipe", None, "seq", None, "tensor"),
        P(None, "tensor"),
        P("tensor"),
        P("tensor"),
        P("seq", "tensor"),
        P(),
    )
    return jax.shard_map(
        per_device,
        mesh=mesh,
        in_specs=placed,
        out_specs=P("pipe", None, "seq", "tensor"),
        check_vma=False,
    )
```
